32 devices in a mesh: row: 4 (over y, core), col: 4 (over z), smp: 2 (over x).
Axes of the slice: x: 2, y: 2, z: 4, core: 2. Of those that a mesh axis runs over, the one named last changes fastest.
Arguments:
- precision: float32 [2048, 2048], P('row', 'col'), as said below
- residuals: float32 [2048, 1024], P(('col', 'row'), 'smp'), may hold values from -6 to 6
- labels: int32 [2048], replicated, may hold values from 0 to 3
Outputs:
- updated: float32 [2048, 2048], P('row', 'col')
The draws below stay inside these ranges and needn't reach their ends.
Inputs may be any that keep to these rules, and one draw needn't show every extreme that they name: `precision`: symmetric; diagonal entries from 1.5 to 3.
All inputs are finite; a program needn't handle non-finite values.
Results may differ from the reference program's by a relative error of at most 0.0003.
Values sent between devices are 32-bit elements; how exact they have to be, the bound alone decides.
No kernel may reach another device: no remote copies, remote signals or barrier semaphores. Data moves between devices by JAX's collectives and lax.ppermute only.
A program may use at most 64 MiB of HBM per device.

```python
import jax
import jax.numpy as jnp
from jax import lax

COMPS = 4
SERIES = 2048
SAMPLES = 1024


def draw_precision(key, part):
    first, second = jax.random.split(jax.random.fold_in(key, 17), 2)
    base = jax.random.normal(first, (SERIES, SERIES), jnp.float32) * (0.5 / SERIES ** 0.5)
    offdiag = (base + base.T) * 0.5 ** 0.5
    diag = jax.random.uniform(second, (SERIES,), jnp.float32, 1.5, 3.0)
    ident = jnp.eye(SERIES, dtype=jnp.float32)
    return offdiag * (1.0 - ident) + ident * diag[:, None]


def plant(drawn, rng, least, high):
    longest = drawn.shape.index(max(drawn.shape))
    spots = []
    for shift in (0, 1):
        where = [jax.random.randint(jax.random.fold_in(rng, axis), (), 0, length) for axis, length in enumerate(drawn.shape)]
        where[longest] = (where[longest] + shift) % drawn.shape[longest]
        spots.append(tuple(where))
    return drawn.at[spots[0]].set(least).at[spots[1]].set(high)


def level_of(stream_key, shape, cuts, smallest, top_value):
    factor_of, own = 1.0, jax.random.fold_in(stream_key, 6)
    for axis_at, parts in cuts:
        heights = jnp.exp(jax.random.uniform(jax.random.fold_in(own, axis_at), (parts,), jnp.float32, smallest / len(cuts), top_value / len(cuts)))
        factor_of = factor_of * jnp.repeat(heights, shape[axis_at] // parts).reshape([-1 if axis == axis_at else 1 for axis in range(len(shape))])
    return factor_of


def bell_draw(stream_key, shape, deviation, most, shards=(), held_as=jnp.bfloat16):
    level = level_of(stream_key, shape, shards, -0.22, 0.18) if shards else 1.0
    array = jax.random.normal(stream_key, shape, jnp.float32) * deviation * level
    return jnp.minimum(jnp.maximum(array, -most), most).astype(held_as)


def setup_inputs(seed: int = 0) -> dict:
    seeds = jax.random.split(jax.random.key(seed), 4)
    precision = draw_precision(jax.random.fold_in(seeds[3], 71), 0)
    residuals = bell_draw(seeds[1], (SERIES, SAMPLES), 1.0, 6.0, ((0, 16), (1, 2)), jnp.float32)
    labels = plant(jax.random.randint(seeds[2], (SERIES,), 0, COMPS), jax.random.fold_in(seeds[2], 1), 0, COMPS - 1).astype(jnp.int32)
    return {"precision": precision, "residuals": residuals, "labels": labels}


STEP_SIZE = 0.5
PENALTY = 0.04


def reference(precision, residuals, labels):
    image = jnp.dot(precision, residuals, precision=lax.Precision.HIGHEST, preferred_element_type=jnp.float32)
    gram = jnp.dot(image, residuals.T, precision=lax.Precision.HIGHEST, preferred_element_type=jnp.float32)
    count = residuals.shape[1]
    ident = jnp.eye(precision.shape[0], dtype=jnp.float32)
    diag = jnp.diagonal(precision)
    gradient = (gram + gram.T) / (2.0 * count) - ident * (1.0 / diag)[:, None]
    moved = precision - STEP_SIZE * gradient
    shrunk = jnp.sign(moved) * jnp.maximum(jnp.abs(moved) - STEP_SIZE * PENALTY, 0.0)
    same = (labels[:, None] == labels[None, :]).astype(jnp.float32)
    return ident * moved + (1.0 - ident) * shrunk * same
```

```python
import jax
import jax.numpy as jnp
from jax import lax
from jax.sharding import PartitionSpec as P

STEP_SIZE = 0.5
PENALTY = 0.04
CORES = 2


def dot(left, right, dims):
    return lax.dot_general(
        left, right, (dims, ((), ())), precision=lax.Precision.HIGH, preferred_element_type=jnp.float32
    )


def ring(value, axis, shift):
    n = lax.axis_size(axis)
    return lax.ppermute(value, axis, [(i, (i + shift) % n) for i in range(n)])


def mate(value):
    n = lax.axis_size("row")
    return lax.ppermute(value, "row", [(i, i ^ 1) for i in range(n)])


def place(total, piece, index):
    return lax.dynamic_update_slice_in_dim(total, piece, index * piece.shape[0], 0)


def take(total, index, rows):
    return lax.dynamic_slice_in_dim(total, index * rows, rows, 0)


def gather_ring(piece, axis):
    n = lax.axis_size(axis)
    far = n // 2
    half = piece.shape[0] // 2
    got = {0: piece}
    up = down = piece
    for step in range(1, far):
        up, down = ring(up, axis, 1), ring(down, axis, -1)
        got[-step], got[step] = up, down
    up, down = ring(up[:half], axis, 1), ring(down[half:], axis, -1)
    got[far] = jnp.concatenate([up, down], axis=0)
    return got


def scatter_ring(whole, axis):
    n = lax.axis_size(axis)
    me = lax.axis_index(axis)
    far = n // 2
    rows = whole.shape[0] // n
    half = rows // 2
    part = lambda d: take(whole, (me + d) % n, rows)
    opposite = part(far)
    up = ring(opposite[:half], axis, 1)
    down = ring(opposite[half:], axis, -1)
    for step in range(far - 1, 0, -1):
        above, below = part(step), part(-step)
        if step == far - 1:
            above = jnp.concatenate([above[:half] + up, above[half:]], axis=0)
            below = jnp.concatenate([below[:half], below[half:] + down], axis=0)
        else:
            above, below = above + up, below + down
        up, down = ring(above, axis, 1), ring(below, axis, -1)
    mine = part(0)
    if far == 1:
        return mine + jnp.concatenate([up, down], axis=0)
    return mine + up + down


def assemble(got, me, n):
    piece = got[0]
    total = jnp.zeros((piece.shape[0] * n, piece.shape[1]), piece.dtype)
    for distance, value in got.items():
        total = place(total, value, (me + distance) % n)
    return total


def broadcast_row(piece, n_row, n_col, row_at, col_at):
    n_y = n_row // CORES
    reach = 1
    while reach < n_y:
        pairs = []
        for col in range(n_col):
            y, core = divmod(col, CORES)
            for offset in range(min(reach, n_y - reach)):
                src = (y + offset) % n_y * CORES + core
                dst = (y + offset + reach) % n_y * CORES + core
                pairs.append((src * n_col + col, dst * n_col + col))
        got = lax.ppermute(piece, ("row", "col"), pairs)
        offset = (row_at // CORES - col_at // CORES) % n_y
        piece = jnp.where((offset >= reach) & (offset < 2 * reach), got, piece)
        reach *= 2
    pairs = []
    for col in range(n_col):
        for y in range(n_y):
            src = y * CORES + col % CORES
            pairs.append((src * n_col + col, (src ^ 1) * n_col + col))
    got = lax.ppermute(piece, ("row", "col"), pairs)
    return jnp.where(row_at % CORES == col_at % CORES, piece, got)


def shards(precision, residuals, labels):
    tile = precision.shape[0]
    n_row, n_col = lax.axis_size("row"), lax.axis_size("col")
    n_y = n_row // CORES
    row_at, col_at = lax.axis_index("row"), lax.axis_index("col")
    y_at, core_at = row_at // CORES, row_at % CORES
    rows = residuals.shape[0]

    x_col = jnp.zeros((tile, residuals.shape[1]), jnp.float32)
    for step in range(n_y):
        value = residuals if step == 0 else ring(residuals, "row", CORES * step)
        source = (row_at - CORES * step) % n_row
        x_col = place(x_col, value, source)
        x_col = place(x_col, mate(value), source ^ 1)

    pieces = assemble(gather_ring(residuals, "col"), col_at, n_col)
    x_row = jnp.zeros((tile, residuals.shape[1]), jnp.float32)
    for step in range(n_y):
        pair = take(pieces, (y_at + step) % n_y, CORES * rows)
        if step:
            pair = ring(pair, "row", CORES * step)
        source = (row_at - CORES * step) % n_row
        x_row = place(x_row, take(pair, core_at, rows), source)
        x_row = place(x_row, mate(take(pair, 1 - core_at, rows)), source ^ 1)

    partial_rows = dot(precision, x_col, ((1,), (0,)))
    got = gather_ring(scatter_ring(partial_rows, "col"), "col")
    y_row = assemble(got, col_at, n_col)

    count = residuals.shape[1] * lax.axis_size("smp")
    row_labels = take(labels, row_at, tile)
    row_ids = row_at * tile + jnp.arange(tile)
    updated = jnp.zeros((tile, tile), jnp.float32)
    for distance, piece in got.items():
        at = (col_at + distance) % n_col
        y_piece = broadcast_row(piece, n_row, n_col, row_at, col_at)
        x_piece = take(x_col, at, rows)
        mine = dot(y_row, x_piece, ((1,), (1,))) + dot(x_row, y_piece, ((1,), (1,)))
        gram = mine + ring(mine, "smp", 1)
        prior = lax.dynamic_slice_in_dim(precision, at * rows, rows, 1)
        col_ids = col_at * tile + at * rows + jnp.arange(rows)
        col_labels = lax.dynamic_slice_in_dim(labels, col_at * tile + at * rows, rows, 0)
        diagonal = row_ids[:, None] == col_ids[None, :]
        recip = jnp.where(diagonal, 1.0 / jnp.where(diagonal, prior, 1.0), 0.0)
        moved = prior - STEP_SIZE * (gram / (2.0 * count) - recip)
        shrunk = jnp.sign(moved) * jnp.maximum(jnp.abs(moved) - STEP_SIZE * PENALTY, 0.0)
        same = row_labels[:, None] == col_labels[None, :]
        chunk = jnp.where(diagonal, moved, jnp.where(same, shrunk, 0.0))
        updated = lax.dynamic_update_slice_in_dim(updated, chunk, at * rows, 1)
    return updated


def solution(mesh):
    return jax.shard_map(
        shards,
        mesh=mesh,
        in_specs=(P("row", "col"), P(("col", "row"), "smp"), P()),
        out_specs=P("row", "col"),
        check_vma=False,
    )
```

```python
import jax
import jax.numpy as jnp
from jax import lax
from jax.sharding import PartitionSpec as P

STEP_SIZE = 0.5
PENALTY = 0.04
CORES = 2


def dot(left, right, dims):
    return lax.dot_general(
        left, right, (dims, ((), ())), precision=lax.Precision.HIGH, preferred_element_type=jnp.float32
    )


def swap(value, axis, mask):
    n = lax.axis_size(axis)
    return lax.ppermute(value, axis, [(i, i ^ mask) for i in range(n)])


def shift(value, axis, by):
    n = lax.axis_size(axis)
    return lax.ppermute(value, axis, [(i, (i + by) % n) for i in range(n)])


def together(*values):
    return lax.optimization_barrier(values)


def cut(value, count):
    size = value.shape[0] // count
    return [value[i * size:(i + 1) * size] for i in range(count)]


def take(total, index, size):
    return lax.dynamic_slice_in_dim(total, index * size, size, 0)


def gather_first(piece, axis, n, unit=1):
    even = [piece]
    if n > 2:
        even, odd = gather_first(piece, axis, n // 2, 2 * unit)
        even = gather_last(even, odd, axis, 2 * unit)
    return even, swap(piece, axis, unit)


def gather_last(even, odd, axis, unit=1):
    odd = [odd]
    if len(even) > 1:
        odd += cut(swap(jnp.concatenate(even[1:], axis=0), axis, unit), len(even) - 1)
    return [value for pair in zip(even, odd) for value in pair]


def shards(precision, residuals, labels):
    tile = precision.shape[0]
    n_row, n_col, n_smp = lax.axis_size("row"), lax.axis_size("col"), lax.axis_size("smp")
    n_y = n_row // CORES
    row_at, col_at, smp_at = lax.axis_index("row"), lax.axis_index("col"), lax.axis_index("smp")
    y_at, core_at = row_at // CORES, row_at % CORES
    rows = residuals.shape[0]
    blocks = [col_at ^ o for o in range(n_col)]

    def by_source(mine, mates, wanted):
        whole = jnp.concatenate(mine + mates, axis=0)
        slots = [(y_at - j // CORES) % n_y + jnp.where(core_at == j % CORES, 0, n_y) for j in wanted]
        return jnp.concatenate([take(whole, slot, rows) for slot in slots], axis=0)

    def split(pairs):
        mine = [take(pair, core_at, rows) for pair in pairs]
        return mine, jnp.concatenate([take(pair, 1 - core_at, rows) for pair in pairs], axis=0)

    def spread(piece_of):
        return [piece_of(y_at)] + [
            shift(piece_of((y_at + step) % n_y), "row", CORES * step) for step in range(1, n_y)
        ]

    def along_row(piece):
        return [piece] + [shift(piece, "row", CORES * step) for step in range(1, n_y)]

    pairs = spread(lambda y: take(precision, y, CORES * rows))
    even, odd = gather_first(residuals, "col", n_col)
    even[-1], odd, pairs[-1] = together(even[-1], odd, pairs[-1])
    x_pieces = gather_last(even, odd, "col")
    mine, others = split(pairs)
    mates = swap(others, "row", 1)
    x_mine = along_row(together(residuals, pairs[-1])[0])
    x_pieces[-1], mates, x_mine[-1] = together(x_pieces[-1], mates, x_mine[-1])
    prior = by_source(mine, cut(mates, n_y), blocks)
    x_all = jnp.concatenate(x_pieces, axis=0)

    image = dot(prior, x_all, ((0,), (0,))).reshape(n_y, CORES, rows, x_all.shape[1])
    got = swap(lax.dynamic_index_in_dim(image, 1 - core_at, 1, keepdims=False), "row", 1)
    image = lax.dynamic_index_in_dim(image, core_at, 1, keepdims=False) + got
    share = lax.dynamic_index_in_dim(image, y_at, 0, keepdims=False)
    for step in range(1, n_y):
        away = lax.dynamic_index_in_dim(image, (y_at + step) % n_y, 0, keepdims=False)
        share = share + shift(away, "row", CORES * step)
    x_mates = [swap(value, "row", 1) for value in x_mine]
    x_col = by_source(x_mine, x_mates, range(n_row))
    y_mine = along_row(share)
    even, odd = gather_first(share, "col", n_col)
    even[-1], odd, y_mine[-1] = together(even[-1], odd, y_mine[-1])
    y_pieces = gather_last(even, odd, "col")
    y_col = by_source(y_mine, [swap(value, "row", 1) for value in y_mine], range(n_row))

    count = residuals.shape[1] * n_smp
    width = tile // n_smp
    row_labels = jnp.concatenate([take(labels, block * n_row + row_at, rows) for block in blocks])
    col_labels = take(labels, col_at * n_smp + smp_at, width)
    prior = lax.dynamic_slice_in_dim(prior, smp_at * width, width, 1)
    row_ids = jnp.arange(tile)[:, None] + row_at * rows
    diagonal = (row_ids == jnp.arange(width)[None, :] + smp_at * width) & (jnp.arange(tile)[:, None] < rows)
    base = prior + jnp.where(diagonal, STEP_SIZE / jnp.where(diagonal, prior, 1.0), 0.0)
    same = row_labels[:, None] == col_labels[None, :]
    bound = jnp.where(diagonal, 0.0, jnp.where(same, STEP_SIZE * PENALTY, jnp.inf))
    updated = []
    near = n_col // 2 + 1 if n_col > 2 else n_col
    for group in [g for g in (range(near), range(near, n_col)) if len(g)]:
        if updated:
            y_pieces[-1] = together(y_pieces[-1], away[-1])[0]
        y_rows = jnp.concatenate([y_pieces[o] for o in group], axis=0)
        x_rows = jnp.concatenate([x_pieces[o] for o in group], axis=0)

        def gram_of(part):
            y_part, x_part = take(y_col, part, width), take(x_col, part, width)
            return dot(y_rows, x_part, ((1,), (1,))) + dot(x_rows, y_part, ((1,), (1,)))

        away = [gram_of((smp_at + step) % n_smp) for step in range(1, n_smp)]
        gram = gram_of(smp_at)
        for step in range(1, n_smp):
            gram = gram + shift(away[step - 1], "smp", step)
        at = slice(group[0] * rows, (group[-1] + 1) * rows)
        moved = base[at] - gram * (STEP_SIZE / (2.0 * count))
        updated.append(moved - jnp.clip(moved, -bound[at], bound[at]))
    updated = jnp.concatenate(updated, axis=0)

    def pair_of(y):
        return jnp.concatenate([take(updated, col_at ^ (CORES * y + k), rows) for k in range(CORES)], axis=0)

    halves = [[] for _ in range(n_smp)]
    pairs = spread(pair_of)
    for step in range(n_y):
        pair = pairs[step]
        both = [take(pair, core_at, rows), swap(take(pair, 1 - core_at, rows), "row", 1)]
        both = jnp.concatenate([take(jnp.concatenate(both, axis=0), core_at ^ k, rows) for k in range(CORES)], axis=0)
        for turn in range(n_smp):
            halves[turn].append(shift(both, "smp", turn) if turn else both)
        if step + 1 < n_y:
            halves[-1][-1], pairs[step + 1] = together(halves[-1][-1], pairs[step + 1])
    whole = jnp.zeros_like(precision)
    for turn, half in enumerate(halves):
        half = jnp.concatenate(half, axis=0)
        half = jnp.concatenate([take(half, (y_at - y) % n_y, CORES * rows) for y in range(n_y)], axis=0)
        whole = lax.dynamic_update_slice_in_dim(whole, half, (smp_at - turn) % n_smp * width, 1)
    return whole


def solution(mesh):
    return jax.shard_map(
        shards,
        mesh=mesh,
        in_specs=(P("row", "col"), P(("col", "row"), "smp"), P()),
        out_specs=P("row", "col"),
        check_vma=False,
    )
```

```python
import jax
import jax.numpy as jnp
from jax import lax
from jax.sharding import PartitionSpec as P

STEP_SIZE = 0.5
PENALTY = 0.04
CORES = 2


def dot(left, right, dims):
    return lax.dot_general(
        left, right, (dims, ((), ())), precision=lax.Precision.HIGH, preferred_element_type=jnp.float32
    )


def swap(value, axis, mask):
    n = lax.axis_size(axis)
    return lax.ppermute(value, axis, [(i, i ^ mask) for i in range(n)])


def shift(value, axis, by):
    n = lax.axis_size(axis)
    return lax.ppermute(value, axis, [(i, (i + by) % n) for i in range(n)])


def together(*values):
    return lax.optimization_barrier(values)


def cut(value, count):
    size = value.shape[0] // count
    return [value[i * size:(i + 1) * size] for i in range(count)]


def take(total, index, size):
    return lax.dynamic_slice_in_dim(total, index * size, size, 0)


def gather_first(piece, axis, n, unit=1):
    even = [piece]
    if n > 2:
        even, odd = gather_first(piece, axis, n // 2, 2 * unit)
        even = gather_last(even, odd, axis, 2 * unit)
    return even, swap(piece, axis, unit)


def gather_last(even, odd, axis, unit=1):
    odd = [odd]
    if len(even) > 1:
        odd += cut(swap(jnp.concatenate(even[1:], axis=0), axis, unit), len(even) - 1)
    return [value for pair in zip(even, odd) for value in pair]


def shards(precision, residuals, labels):
    tile = precision.shape[0]
    n_row, n_col, n_smp = lax.axis_size("row"), lax.axis_size("col"), lax.axis_size("smp")
    n_y = n_row // CORES
    row_at, col_at, smp_at = lax.axis_index("row"), lax.axis_index("col"), lax.axis_index("smp")
    y_at, core_at = row_at // CORES, row_at % CORES
    rows = residuals.shape[0]
    offsets = [*range(0, n_col, 2), *range(1, n_col, 2)]
    blocks = [col_at ^ o for o in offsets]

    def by_source(mine, mates, wanted):
        whole = jnp.concatenate(mine + mates, axis=0)
        slots = [(y_at - j // CORES) % n_y + jnp.where(core_at == j % CORES, 0, n_y) for j in wanted]
        return jnp.concatenate([take(whole, slot, rows) for slot in slots], axis=0)

    def split(pairs):
        mine = [take(pair, core_at, rows) for pair in pairs]
        return mine, jnp.concatenate([take(pair, 1 - core_at, rows) for pair in pairs], axis=0)

    def spread(piece_of):
        return [piece_of(y_at)] + [
            shift(piece_of((y_at + step) % n_y), "row", CORES * step) for step in range(1, n_y)
        ]

    def along_row(piece):
        return [piece] + [shift(piece, "row", CORES * step) for step in range(1, n_y)]

    even, odd = gather_first(residuals, "col", n_col)
    x_mine = along_row(residuals)
    even[-1], odd, x_mine[-1] = together(even[-1], odd, x_mine[-1])
    x_pieces = gather_last(even, odd, "col")
    by_core = precision.reshape(n_y, CORES, rows, tile)
    kept = lax.dynamic_index_in_dim(by_core, core_at, 1, keepdims=False)
    came = swap(lax.dynamic_index_in_dim(by_core, 1 - core_at, 1, keepdims=False), "row", 1)

    def both_of(y):
        here = [lax.dynamic_index_in_dim(value, y, 0, keepdims=False) for value in (kept, came)]
        return jnp.concatenate(here, axis=0)

    pairs = spread(both_of)
    x_pieces[-1], pairs[-1] = together(x_pieces[-1], pairs[-1])
    mine, mates = zip(*[cut(pair, CORES) for pair in pairs])
    prior = by_source(list(mine), list(mates), blocks)
    x_all = jnp.concatenate([x_pieces[o] for o in offsets], axis=0)

    image = dot(prior, x_all, ((0,), (0,))).reshape(n_y, CORES, rows, x_all.shape[1])
    got = swap(lax.dynamic_index_in_dim(image, 1 - core_at, 1, keepdims=False), "row", 1)
    image = lax.dynamic_index_in_dim(image, core_at, 1, keepdims=False) + got
    share = lax.dynamic_index_in_dim(image, y_at, 0, keepdims=False)
    for step in range(1, n_y):
        away = lax.dynamic_index_in_dim(image, (y_at + step) % n_y, 0, keepdims=False)
        share = share + shift(away, "row", CORES * step)
    x_mates = [swap(value, "row", 1) for value in x_mine]
    x_col = by_source(x_mine, x_mates, range(n_row))
    even, odd = gather_first(share, "col", n_col)
    y_mine = along_row(together(share, x_col)[0])
    even[-1], odd, y_mine[-1] = together(even[-1], odd, y_mine[-1])
    y_pieces = gather_last(even, odd, "col")
    y_col = by_source(y_mine, [swap(value, "row", 1) for value in y_mine], range(n_row))

    count = residuals.shape[1] * n_smp
    width = tile // n_smp
    row_labels = jnp.concatenate([take(labels, block * n_row + row_at, rows) for block in blocks])
    col_labels = take(labels, col_at * n_smp + smp_at, width)
    prior = lax.dynamic_slice_in_dim(prior, smp_at * width, width, 1)
    row_ids = jnp.arange(tile)[:, None] + row_at * rows
    diagonal = (row_ids == jnp.arange(width)[None, :] + smp_at * width) & (jnp.arange(tile)[:, None] < rows)
    base = prior + jnp.where(diagonal, STEP_SIZE / jnp.where(diagonal, prior, 1.0), 0.0)
    same = row_labels[:, None] == col_labels[None, :]
    bound = jnp.where(diagonal, 0.0, jnp.where(same, STEP_SIZE * PENALTY, jnp.inf))
    part = tile // CORES
    groups, last = [], None
    for at in (slice(0, part), slice(part, tile)):
        if groups:
            y_pieces[-1] = together(y_pieces[-1], last)[0]
        y_rows = jnp.concatenate([y_pieces[o] for o in offsets[at.start // rows:at.stop // rows]], axis=0)
        x_rows = x_all[at]

        def gram_of(turn):
            y_part, x_part = take(y_col, turn, width), take(x_col, turn, width)
            return dot(y_rows, x_part, ((1,), (1,))) + dot(x_rows, y_part, ((1,), (1,)))

        away = [gram_of((smp_at + turn) % n_smp) for turn in range(1, n_smp)]
        gram = gram_of(smp_at)
        for turn in range(1, n_smp):
            gram = gram + shift(away[turn - 1], "smp", turn)
        last = away[-1]
        moved = base[at] - gram * (STEP_SIZE / (2.0 * count))
        groups.append(moved - jnp.clip(moved, -bound[at], bound[at]))

    def turned(pieces):
        return [shift(jnp.concatenate(pieces, axis=0), "smp", turn) for turn in range(1, n_smp)]

    sent, joined, waiting = [], [[] for _ in range(n_smp)], []
    for updated in groups:
        pieces = []
        for step in range(n_y):
            piece = take(updated, (col_at // CORES) ^ ((y_at + step) % n_y), rows)
            pieces.append(shift(piece, "row", CORES * step) if step else piece)
        came = turned(waiting + pieces[:1])
        came[-1], pieces[-1] = together(came[-1], pieces[-1])
        for turn in range(1, n_smp):
            joined[turn].append(came[turn - 1])
        waiting = pieces[1:]
        joined[0] += pieces
    for turn, value in enumerate(turned(waiting), 1):
        joined[turn].append(value)
    halves = []
    for value in joined:
        value = jnp.concatenate(value, axis=0)
        mine = take(value, (core_at + col_at) % CORES, part)
        mates = swap(take(value, 1 - (core_at + col_at) % CORES, part), "row", 1)
        halves.append(by_source(cut(mine, n_y), cut(mates, n_y), range(n_row)))
    whole = jnp.zeros_like(precision)
    for turn, half in enumerate(halves):
        whole = lax.dynamic_update_slice_in_dim(whole, half, (smp_at - turn) % n_smp * width, 1)
    return whole


def solution(mesh):
    return jax.shard_map(
        shards,
        mesh=mesh,
        in_specs=(P("row", "col"), P(("col", "row"), "smp"), P()),
        out_specs=P("row", "col"),
        check_vma=False,
    )
```
